32 devices in a mesh: members: 2 (over x), lon: 16 (over z, y, core).
Axes of the slice: x: 2, y: 2, z: 4, core: 2. Of those that a mesh axis runs over, the one named last changes fastest.
Arguments:
- state: bfloat16 [262144, 128], P(('members', 'lon')), parts along dimension 0, may hold values from -6 to 6
- cotangent: bfloat16 [262144, 128], P(('members', 'lon')), parts along dimension 0, may hold values from -6 to 6
- local_interp: bfloat16 [2048, 128, 128], P(('members', 'lon')), parts along dimension 0, may hold values from -0.5 to 0.5
- remote_interp: bfloat16 [384, 128, 128], P(('members', 'lon')), parts along dimension 0, may hold values from -0.5 to 0.5
- departures: int32 [3, 384], P(None, ('members', 'lon')), parts along dimension 1, may hold values from 0 to 63, as said below
- counts: int32 [32], P(('members', 'lon')), parts along dimension 0, may hold values from 3 to 12, as said below
- w_in: bfloat16 [128, 256], replicated, may hold values from -0.5 to 0.5
- b_in: float32 [256], replicated, may hold values from -4 to 4
- w_out: bfloat16 [256, 128], replicated, may hold values from -0.375 to 0.375
Outputs:
- grad_state: bfloat16 [262144, 128], P(('members', 'lon')), parts along dimension 0
- grad_w_in: float32 [256, 256], P('members'), parts along dimension 0
- grad_b_in: float32 [512], P('members'), parts along dimension 0
- grad_w_out: float32 [512, 128], P('members'), parts along dimension 0
The draws below stay inside these ranges and needn't reach their ends.
There are 2 independent parts, one for each index of `members`. The reference program is written for one: setup_inputs(seed, part) draws one part's arguments, and reference() takes and returns one part's arrays. A program takes and returns all parts, laid end to end along the dimension named above; an argument that names none is the same for every part. Nothing has to cross between parts.
Inputs may be any that keep to these rules, and one draw needn't show every extreme that they name: `departures`: A live entry's source tile lies within 3 sectors of its own tile, cyclically in longitude. Among the live entries of one tile at most 2 name one source tile, and every draw has a tile where that most is reached. Blocks are block numbers within a tile. `counts`: some tile uses all 12 entries.
All inputs are finite; a program needn't handle non-finite values.
Results may differ from the reference program's by a relative error of at most 0.0068.
Values may be sent and summed in bfloat16 or wider, within the bound.
A program may use at most 64 MiB of HBM per device.

```python
import jax
import jax.numpy as jnp
from jax import lax

FEAT = 128
HIDDEN_SIZE = 256
BLOCK_COLS = 128
BLOCKS_DEV = 64
ENTRIES = 12
CAP = 2
REACH = 3
TILES = 16
COLUMNS = 131072
N_LON = 16


def draw_departures(key, part):
    key = jax.random.fold_in(key, 11)
    first, second, third = jax.random.split(key, 3)
    tiles = N_LON
    slots = (2 * REACH + 1) * CAP
    offsets = jnp.repeat(jnp.arange(-REACH, REACH + 1, dtype=jnp.int32), CAP)
    scores = jax.random.randint(first, (tiles, slots), 0, 1 << 20) * slots + jnp.arange(slots, dtype=jnp.int32)[None, :]
    order = jnp.argsort(scores, axis=1)
    chosen = offsets[order][:, :ENTRIES]
    owners = jnp.arange(tiles, dtype=jnp.int32)[:, None]
    sources = (owners + chosen + tiles) % tiles
    source_blocks = jax.random.randint(second, (tiles, ENTRIES), 0, BLOCKS_DEV)
    targets = jax.random.randint(third, (tiles, ENTRIES), 0, BLOCKS_DEV)
    return jnp.stack([sources, source_blocks, targets]).reshape(3, tiles * ENTRIES).astype(jnp.int32)


def draw_counts(key, part):
    key = jax.random.fold_in(key, 23)
    first, second = jax.random.split(key)
    drawn = jax.random.randint(first, (N_LON,), ENTRIES // 4, ENTRIES + 1)
    picked = jax.random.randint(second, (), 0, N_LON)
    return jnp.where(jnp.arange(N_LON) == picked, ENTRIES, drawn).astype(jnp.int32)


def levels(key, extent, shards, least, high):
    def one(axis_at, parts):
        draws = jax.random.uniform(jax.random.fold_in(jax.random.fold_in(key, 6), axis_at), (parts,), jnp.float32, least / len(shards), high / len(shards))
        return jnp.repeat(jnp.exp(draws), extent[axis_at] // parts).reshape((-1,) + (1,) * (len(extent) - axis_at - 1))

    gain = one(*shards[0])
    for cut in shards[1:]:
        gain = gain * one(*cut)
    return gain


def bell_draw(own_key, dims, spread, bound, cuts=(), kind=jnp.bfloat16):
    result = spread * jax.random.normal(own_key, dims, jnp.float32)
    if cuts:
        result = result * levels(own_key, dims, cuts, -0.22, 0.18)
    return jnp.clip(result, -bound, bound).astype(kind)


def setup_inputs(seed: int = 0, part: int = 0) -> dict:
    key_of = jax.random.split(jax.random.key(seed), 10)
    own_keys = jax.random.split(jax.random.fold_in(key_of[9], part), 10)
    return {
        "state": bell_draw(own_keys[0], (COLUMNS, FEAT), 1.0, 6.0, ((0, 16),)),
        "cotangent": bell_draw(own_keys[1], (COLUMNS, FEAT), 1.0, 6.0, ((0, 16),)),
        "local_interp": bell_draw(own_keys[2], (TILES * BLOCKS_DEV, BLOCK_COLS, BLOCK_COLS), BLOCK_COLS ** -0.5, 0.5, ((0, 16),)),
        "remote_interp": bell_draw(own_keys[3], (TILES * ENTRIES, BLOCK_COLS, BLOCK_COLS), BLOCK_COLS ** -0.5, 0.5, ((0, 16),)),
        "departures": draw_departures(jax.random.fold_in(jax.random.fold_in(key_of[9], part), 71), part),
        "counts": draw_counts(jax.random.fold_in(jax.random.fold_in(key_of[9], part), 71), part),
        "w_in": bell_draw(key_of[6], (FEAT, HIDDEN_SIZE), FEAT ** -0.5, 0.5),
        "b_in": bell_draw(key_of[7], (HIDDEN_SIZE,), 1.0, 4.0, (), jnp.float32),
        "w_out": bell_draw(key_of[8], (HIDDEN_SIZE, FEAT), HIDDEN_SIZE ** -0.5, 0.375),
    }


def reference(state, cotangent, local_interp, remote_interp, departures, counts, w_in, b_in, w_out):
    tiles = N_LON
    blocks = state.reshape(tiles, BLOCKS_DEV, BLOCK_COLS, FEAT)
    sources = departures[0].reshape(tiles, ENTRIES)
    source_blocks = departures[1].reshape(tiles, ENTRIES)
    targets = departures[2].reshape(tiles, ENTRIES)
    lives = jnp.arange(ENTRIES, dtype=jnp.int32)[None, :] < counts[:, None]
    local_w = local_interp.reshape(tiles, BLOCKS_DEV, BLOCK_COLS, BLOCK_COLS)
    remote_w = remote_interp.reshape(tiles, ENTRIES, BLOCK_COLS, BLOCK_COLS)
    cots = cotangent.reshape(tiles, BLOCKS_DEV * BLOCK_COLS, FEAT)

    def one_tile(items):
        lw, rw, srcs, sblks, dsts, alive, own, grads = items
        weight = alive.astype(jnp.float32)[:, None, None]
        yfull = jnp.einsum("tcd,tdf->tcf", lw.astype(jnp.float32), own.astype(jnp.float32))
        picked = blocks[srcs, sblks]
        contrib = jnp.einsum("ecd,edf->ecf", rw.astype(jnp.float32), picked.astype(jnp.float32)) * weight
        where_to = jnp.where(alive, dsts, BLOCKS_DEV).astype(jnp.int32)
        yfull = yfull.at[where_to].add(contrib, mode="drop")
        y_b = yfull.astype(jnp.bfloat16).reshape(BLOCKS_DEV * BLOCK_COLS, FEAT)
        pre = jnp.dot(y_b, w_in, preferred_element_type=jnp.float32) + b_in
        hidden = jnp.tanh(pre)
        h_b = hidden.astype(jnp.bfloat16)
        ghid = jnp.dot(grads, w_out.T, preferred_element_type=jnp.float32)
        gpre = ghid * (1.0 - hidden * hidden)
        gpre_b = gpre.astype(jnp.bfloat16)
        gyfull = grads.astype(jnp.float32) + jnp.dot(gpre_b, w_in.T, preferred_element_type=jnp.float32)
        gy_b = gyfull.astype(jnp.bfloat16).reshape(BLOCKS_DEV, BLOCK_COLS, FEAT)
        d_in = jnp.dot(y_b.T, gpre_b, preferred_element_type=jnp.float32)
        d_b = jnp.sum(gpre, axis=0)
        d_out = jnp.dot(h_b.T, grads, preferred_element_type=jnp.float32)
        local_back = jnp.einsum("tdc,tdf->tcf", lw.astype(jnp.float32), gy_b.astype(jnp.float32))
        remote_back = jnp.einsum("edc,edf->ecf", rw.astype(jnp.float32), gy_b[dsts].astype(jnp.float32)) * weight
        return local_back, remote_back, d_in, d_b, d_out

    local_back, remote_back, d_in, d_b, d_out = lax.map(
        one_tile, (local_w, remote_w, sources, source_blocks, targets, lives, blocks, cots))
    total = local_back.at[sources.reshape(-1), source_blocks.reshape(-1)].add(
        remote_back.reshape(tiles * ENTRIES, BLOCK_COLS, FEAT))
    grad_state = total.reshape(COLUMNS, FEAT).astype(jnp.bfloat16)
    return grad_state, jnp.sum(d_in, axis=0), jnp.sum(d_b, axis=0), jnp.sum(d_out, axis=0)
```

```python
import functools

import jax
import jax.numpy as jnp
from jax import lax
from jax.experimental import pallas as pl
from jax.experimental.pallas import tpu as pltpu
from jax.sharding import PartitionSpec as P

CAP = 2
REACH = 3
SPAN = 2 * REACH + 1
SLOTS = SPAN * CAP
GROUP = 16
CHUNK = 4
MESH = pl.DeviceIdType.MESH
F32 = jnp.float32
BF16 = jnp.bfloat16


def mm(a, b):
    return jnp.dot(a, b, preferred_element_type=F32)


def mm_nt(a, b):
    return lax.dot_general(a, b, (((1,), (1,)), ((), ())), preferred_element_type=F32)


def mm_tn(a, b):
    return lax.dot_general(a, b, (((0,), (0,)), ((), ())), preferred_element_type=F32)


def kernel(
    tiles,
    dep, cnt, w_in, b_in, w_out, state_h, cot_h, local_h, remote_h,
    grad_h, din_o, db_o, dout_o,
    state, cot, local, remote, gy, back, result,
    sendbox, fetched, outbox, returned, acc, racc, ysp, csp,
    gsum, dbsum, gout, gin, red, gall, dbin, xin,
    ask_out, ask_in, spec_v, own_v,
    ask_s, spec_s, own_s, spot_s, prev_s, ent_s, last_s,
    in_sem, chunk_sem, out_sem, small_sem,
    ask_send, ask_recv, fet_send, fet_recv, ret_send, ret_recv,
    rs_send, rs_recv, db_send, db_recv, ag_send, ag_recv, x_send, x_recv,
):
    nblocks, width, feat = state.shape
    entries = remote.shape[0]
    nchunks = nblocks // CHUNK
    rows = CHUNK * width
    me = lax.axis_index("lon")
    group = min(GROUP, tiles)
    groups = tiles // group
    part = gout.shape[1]

    def peer_at(offset):
        return lax.rem(me + offset + tiles, tiles)

    load_state = pltpu.make_async_copy(state_h, state, in_sem.at[0])
    load_remote = pltpu.make_async_copy(remote_h, remote, in_sem.at[1])
    load_state.start()

    def load_chunk(c):
        at = pl.ds(c * CHUNK, CHUNK)
        return (
            pltpu.make_async_copy(local_h.at[at], local.at[at], chunk_sem.at[0, c]),
            pltpu.make_async_copy(cot_h.at[at], cot.at[at], chunk_sem.at[1, c]),
        )

    @pl.loop(0, nchunks)
    def _(c):
        for copy in load_chunk(c):
            copy.start()

    load_remote.start()

    barrier = pltpu.get_barrier_semaphore()

    @pl.loop(1, tiles)
    def _(i):
        pl.semaphore_signal(barrier, inc=1, device_id={"lon": peer_at(i)}, device_id_type=MESH)

    count = cnt[0]
    keys, dests, spots = [], [], []
    for e in range(entries):
        ahead = dep[0, e] - me + REACH
        ahead = jnp.where(ahead < 0, ahead + tiles, ahead)
        ahead = jnp.where(ahead >= tiles, ahead - tiles, ahead)
        alive = e < count
        keys.append(jnp.where(alive, ahead, -1))
        dests.append(jnp.where(alive, dep[2, e], -1))
        rank = jnp.int32(0)
        prev = jnp.int32(0)
        for q in range(e):
            rank = rank + jnp.where(keys[q] == keys[e], 1, 0)
            prev = jnp.where(dests[q] == dests[e], q + 1, prev)
        spots.append(jnp.where(alive, ahead * CAP + rank, SLOTS))
        spot_s[e] = spots[e]
        prev_s[e] = prev
    line = lax.broadcasted_iota(jnp.int32, (8, 128), 0)
    lane = lax.broadcasted_iota(jnp.int32, (8, 128), 1)
    tile = jnp.full((8, 128), -1, jnp.int32)
    place = jnp.where(lane < CAP, line * CAP + lane, -1)
    slot_entry = jnp.full((8, 128), entries, jnp.int32)
    special = jnp.zeros((8, 128), jnp.int32)
    for e in range(entries):
        tile = jnp.where(place == spots[e], dep[1, e], tile)
        slot_entry = jnp.where(lane == spots[e], e, slot_entry)
        special = jnp.where(lane == dests[e], e + 1, special)
    ask_out[...] = tile
    ask_in[REACH] = tile
    spec_v[0] = special
    spec_v[1] = slot_entry
    spec_copy = pltpu.make_async_copy(spec_v, spec_s, small_sem.at[0])
    spec_copy.start()
    acc[0] = jnp.zeros((width, feat), F32)
    racc[0] = jnp.zeros((width, feat), F32)
    gsum[...] = jnp.zeros_like(gsum)
    dbsum[...] = jnp.zeros_like(dbsum)

    pl.semaphore_wait(barrier, tiles - 1)

    def ask_copy(r):
        return pltpu.make_async_remote_copy(
            src_ref=ask_out, dst_ref=ask_in.at[r],
            send_sem=ask_send.at[r], recv_sem=ask_recv.at[r],
            device_id={"lon": peer_at(r - REACH)}, device_id_type=MESH)

    def fetch_copy(r):
        at = pl.ds(r * CAP, CAP)
        return pltpu.make_async_remote_copy(
            src_ref=sendbox.at[at], dst_ref=fetched.at[at],
            send_sem=fet_send.at[r], recv_sem=fet_recv.at[r],
            device_id={"lon": peer_at(REACH - r)}, device_id_type=MESH)

    def return_copy(r):
        at = pl.ds(r * CAP, CAP)
        return pltpu.make_async_remote_copy(
            src_ref=outbox.at[at], dst_ref=returned.at[at],
            send_sem=ret_send.at[r], recv_sem=ret_recv.at[r],
            device_id={"lon": peer_at(r - REACH)}, device_id_type=MESH)

    others = [r for d in range(REACH, 0, -1) for r in (REACH - d, REACH + d)]
    for r in others:
        ask_copy(r).start()

    def network(y32, ct_ref, base, marks):
        y_b = y32.astype(BF16)
        ct = ct_ref[pl.ds(base, CHUNK)].reshape(rows, feat)
        pre = mm(y_b, w_in[...]) + b_in[...]
        hidden = jnp.tanh(pre)
        h_b = hidden.astype(BF16)
        ghid = mm_nt(ct, w_out[...])
        gpre = ghid * (1.0 - hidden * hidden)
        gpre_b = gpre.astype(BF16)
        ct32 = ct.astype(F32)
        out = (ct32 + mm_nt(gpre_b, w_in[...])).astype(BF16)
        y_m, ct_m, db = [], [], None
        for i in range(CHUNK):
            at = slice(i * width, (i + 1) * width)
            y_m.append((y32[at] * marks[i]).astype(BF16))
            ct_m.append((ct32[at] * marks[i]).astype(BF16))
            here = jnp.sum(gpre[at].reshape(width // 8, 8, -1), axis=0) * marks[i]
            db = here if db is None else db + here
        gsum[:feat] += mm_tn(jnp.concatenate(y_m, axis=0), gpre_b)
        gsum[feat:] += mm_tn(jnp.concatenate(ct_m, axis=0), h_b)
        dbsum[...] += db
        return out.reshape(CHUNK, width, feat)

    def step(c, carry):
        for copy in load_chunk(c):
            copy.wait()
        y, marks = [], []
        for i in range(CHUNK):
            t = c * CHUNK + i
            y.append(mm(local[t], state[t]))
            marks.append(jnp.where(spec_s[0, 0, t] == 0, 1.0, 0.0).astype(F32))
        gy[pl.ds(c * CHUNK, CHUNK)] = network(jnp.concatenate(y, axis=0), cot, c * CHUNK, marks)
        return carry

    spec_copy.wait()
    load_state.wait()
    first = min(2, nchunks)
    second = min(3, nchunks)
    lax.fori_loop(0, first, step, 0)

    for r in others:
        ask_copy(r).wait_recv()
    asked_copy = pltpu.make_async_copy(ask_in, ask_s, small_sem.at[1])
    asked_copy.start()
    lax.fori_loop(first, second, step, 0)
    asked_copy.wait()

    asked = []
    for r in range(SPAN):
        for c in range(CAP):
            asked.append(ask_s[r, r, c])
    for r in others + [REACH]:
        for c in range(CAP):
            k = r * CAP + c
            block = state[jnp.clip(asked[k], 0, nblocks - 1)]
            if r == REACH:
                fetched[k] = block
            else:
                sendbox[k] = block
        if r != REACH:
            fetch_copy(r).start()
    owners = jnp.zeros((8, 128), jnp.int32)
    for k in range(SLOTS):
        last = jnp.int32(0)
        for q in range(k):
            last = jnp.where(asked[q] == asked[k], q + 1, last)
        last_s[k] = last
        owners = jnp.where(lane == asked[k], k + 1, owners)
    own_v[...] = owners
    own_copy = pltpu.make_async_copy(own_v, own_s, small_sem.at[2])
    own_copy.start()

    lax.fori_loop(second, nchunks, step, 0)

    load_remote.wait()
    for r in others:
        fetch_copy(r).wait_recv()

    @pl.loop(0, entries)
    def _(e):
        spot = spot_s[e]
        weight = jnp.where(spot < SLOTS, 1.0, 0.0).astype(F32)
        total = mm(remote[e], fetched[jnp.minimum(spot, SLOTS - 1)]) * weight + acc[prev_s[e]]
        acc[e + 1] = total
        d = dep[2, e]
        ysp[e] = mm(local[d], state[d]) + total
        csp[e] = cot[d]

    @pl.loop(0, entries // CHUNK)
    def _(c):
        marks = []
        for i in range(CHUNK):
            e = c * CHUNK + i
            marks.append(jnp.where(spec_s[0, 0, dep[2, e]] == e + 1, 1.0, 0.0).astype(F32))
        y32 = ysp[pl.ds(c * CHUNK, CHUNK)].reshape(rows, feat)
        gy[pl.ds(nblocks + c * CHUNK, CHUNK)] = network(y32, csp, c * CHUNK, marks)

    for r in others + [REACH]:
        for c in range(CAP):
            k = r * CAP + c
            e = jnp.minimum(spec_s[1, 0, k], entries - 1)
            at = jnp.maximum(spec_s[0, 0, dep[2, e]] - 1, 0) + nblocks
            value = mm_tn(remote[e], gy[at]).astype(BF16)
            if r == REACH:
                returned[k] = value
            else:
                outbox[k] = value
        if r != REACH:
            return_copy(r).start()

    mine = lax.rem(me, group)
    base = me - mine
    gout[...] = gsum[...].astype(BF16).reshape(gout.shape)
    dbin[me] = jnp.sum(dbsum[...], axis=0, keepdims=True)

    def mate(i):
        return lax.rem(mine + i, group)

    def share_copy(i):
        return pltpu.make_async_remote_copy(
            src_ref=gout.at[mate(i)], dst_ref=gin.at[i],
            send_sem=rs_send.at[i], recv_sem=rs_recv.at[i],
            device_id={"lon": base + mate(i)}, device_id_type=MESH)

    def bias_copy(i):
        return pltpu.make_async_remote_copy(
            src_ref=dbin.at[me], dst_ref=dbin.at[me],
            send_sem=db_send.at[i], recv_sem=db_recv.at[i],
            device_id={"lon": peer_at(i)}, device_id_type=MESH)

    def gather_copy(i):
        return pltpu.make_async_remote_copy(
            src_ref=red, dst_ref=gall.at[mine],
            send_sem=ag_send.at[i], recv_sem=ag_recv.at[i],
            device_id={"lon": base + mate(i)}, device_id_type=MESH)

    def cross_copy(i):
        return pltpu.make_async_remote_copy(
            src_ref=xin.at[me // group], dst_ref=xin.at[me // group],
            send_sem=x_send.at[i], recv_sem=x_recv.at[i],
            device_id={"lon": peer_at(i * group)}, device_id_type=MESH)

    @pl.loop(1, group)
    def _(i):
        share_copy(i).start()

    @pl.loop(1, tiles)
    def _(i):
        bias_copy(i).start()

    @pl.loop(0, nchunks)
    def _(c):
        for i in range(CHUNK):
            t = c * CHUNK + i
            s = spec_s[0, 0, t]
            back[t] = mm_tn(local[t], gy[jnp.where(s == 0, t, nblocks + s - 1)])

    @pl.loop(1, group)
    def _(i):
        share_copy(i).wait_recv()

    share = gsum[pl.ds(pl.multiple_of(mine * part, part), part)]
    share = lax.fori_loop(1, group, lambda i, s: s + gin[i].astype(F32), share)
    if groups > 1:
        xin[me // group] = share.astype(BF16)

        @pl.loop(1, groups)
        def _(i):
            cross_copy(i).start()

        @pl.loop(1, groups)
        def _(i):
            cross_copy(i).wait()

        share = lax.fori_loop(
            0, groups, lambda i, s: s + xin[i].astype(F32), jnp.zeros(share.shape, F32))
    red[...] = share.astype(BF16)
    gall[mine] = share.astype(BF16)

    @pl.loop(1, group)
    def _(i):
        gather_copy(i).start()

    own_copy.wait()
    for r in others:
        return_copy(r).wait_recv()
    for k in range(SLOTS):
        weight = jnp.where(asked[k] >= 0, 1.0, 0.0).astype(F32)
        racc[k + 1] = returned[k].astype(F32) * weight + racc[last_s[k]]

    def store_chunk(c):
        at = pl.ds(c * CHUNK, CHUNK)
        return pltpu.make_async_copy(result.at[at], grad_h.at[at], out_sem.at[c])

    @pl.loop(0, nchunks)
    def _(c):
        for i in range(CHUNK):
            t = c * CHUNK + i
            result[t] = (back[t] + racc[own_s[0, t]]).astype(BF16)
        store_chunk(c).start()

    @pl.loop(1, tiles)
    def _(i):
        bias_copy(i).wait()

    db_o[...] = lax.fori_loop(1, tiles, lambda i, s: s + dbin[i], dbin[0])

    @pl.loop(1, group)
    def _(i):
        share_copy(i).wait_send()
        gather_copy(i).wait()

    whole = gall[...].astype(F32).reshape(2 * feat, -1)
    din_o[...] = whole[:feat]
    dout_o[...] = whole[feat:].T

    for r in others:
        ask_copy(r).wait_send()
        fetch_copy(r).wait_send()
        return_copy(r).wait_send()

    @pl.loop(0, nchunks)
    def _(c):
        store_chunk(c).wait()


def body(tiles, state, cotangent, local_interp, remote_interp, departures, counts, w_in, b_in, w_out):
    nblocks, width, _ = local_interp.shape
    feat = state.shape[1]
    hid = w_in.shape[1]
    entries = remote_interp.shape[0]
    nchunks = nblocks // CHUNK
    group = min(GROUP, tiles)
    part = 2 * feat // group
    dma = pltpu.SemaphoreType.DMA
    vmem = pl.BlockSpec(memory_space=pltpu.VMEM)
    smem = pl.BlockSpec(memory_space=pltpu.SMEM)
    hbm = pl.BlockSpec(memory_space=pl.ANY)
    blk = (width, feat)
    grad, d_in, d_b, d_out = pl.pallas_call(
        functools.partial(kernel, tiles),
        out_shape=(
            jax.ShapeDtypeStruct((nblocks,) + blk, BF16),
            jax.ShapeDtypeStruct((feat, hid), F32),
            jax.ShapeDtypeStruct((1, hid), F32),
            jax.ShapeDtypeStruct((hid, feat), F32),
        ),
        in_specs=[smem, smem, vmem, vmem, vmem, hbm, hbm, hbm, hbm],
        out_specs=(hbm, vmem, vmem, vmem),
        scratch_shapes=[
            pltpu.VMEM((nblocks,) + blk, BF16),
            pltpu.VMEM((nblocks,) + blk, BF16),
            pltpu.VMEM((nblocks, width, width), BF16),
            pltpu.VMEM((entries, width, width), BF16),
            pltpu.VMEM((nblocks + entries,) + blk, BF16),
            pltpu.VMEM((nblocks,) + blk, F32),
            pltpu.VMEM((nblocks,) + blk, BF16),
            pltpu.VMEM((SLOTS,) + blk, BF16),
            pltpu.VMEM((SLOTS,) + blk, BF16),
            pltpu.VMEM((SLOTS,) + blk, BF16),
            pltpu.VMEM((SLOTS,) + blk, BF16),
            pltpu.VMEM((entries + 1,) + blk, F32),
            pltpu.VMEM((SLOTS + 1,) + blk, F32),
            pltpu.VMEM((entries,) + blk, F32),
            pltpu.VMEM((entries,) + blk, BF16),
            pltpu.VMEM((2 * feat, hid), F32),
            pltpu.VMEM((8, hid), F32),
            pltpu.VMEM((group, part, hid), BF16),
            pltpu.VMEM((group, part, hid), BF16),
            pltpu.VMEM((part, hid), BF16),
            pltpu.VMEM((group, part, hid), BF16),
            pltpu.VMEM((tiles, 1, hid), F32),
            pltpu.VMEM((tiles // group, part, hid), BF16),
            pltpu.VMEM((8, 128), jnp.int32),
            pltpu.VMEM((SPAN, 8, 128), jnp.int32),
            pltpu.VMEM((2, 8, 128), jnp.int32),
            pltpu.VMEM((8, 128), jnp.int32),
            pltpu.SMEM((SPAN, 8, 128), jnp.int32),
            pltpu.SMEM((2, 8, 128), jnp.int32),
            pltpu.SMEM((8, 128), jnp.int32),
            pltpu.SMEM((entries,), jnp.int32),
            pltpu.SMEM((entries,), jnp.int32),
            pltpu.SMEM((SLOTS,), jnp.int32),
            pltpu.SMEM((SLOTS,), jnp.int32),
            dma((2,)), dma((2, nchunks)), dma((nchunks,)), dma((3,)),
            dma((SPAN,)), dma((SPAN,)), dma((SPAN,)), dma((SPAN,)), dma((SPAN,)), dma((SPAN,)),
            dma((group,)), dma((group,)), dma((tiles,)), dma((tiles,)),
            dma((group,)), dma((group,)),
            dma((max(tiles // group, 2),)), dma((max(tiles // group, 2),)),
        ],
        compiler_params=pltpu.CompilerParams(
            collective_id=0, has_side_effects=True, vmem_limit_bytes=48 * 1024 * 1024
        ),
    )(
        departures, counts, w_in, b_in.reshape(1, hid), w_out,
        state.reshape(nblocks, width, feat), cotangent.reshape(nblocks, width, feat),
        local_interp, remote_interp,
    )
    return grad.reshape(nblocks * width, feat), d_in, d_b.reshape(hid), d_out


def solution(mesh):
    return jax.shard_map(
        functools.partial(body, mesh.shape["lon"]),
        mesh=mesh,
        in_specs=(
            P(("members", "lon"), None),
            P(("members", "lon"), None),
            P(("members", "lon"), None, None),
            P(("members", "lon"), None, None),
            P(None, ("members", "lon")),
            P(("members", "lon")),
            P(),
            P(),
            P(),
        ),
        out_specs=(
            P(("members", "lon"), None),
            P("members", None),
            P("members"),
            P("members", None),
        ),
        check_vma=False,
    )
```

```python
import functools

import jax
import jax.numpy as jnp
from jax import lax
from jax.experimental import pallas as pl
from jax.experimental.pallas import tpu as pltpu
from jax.sharding import PartitionSpec as P

CAP = 2
REACH = 3
SPAN = 2 * REACH + 1
OFFSETS = [0] + [sign * d for d in range(1, REACH + 1) for sign in (-1, 1)]
SLOTS = SPAN * CAP
GROUP = 16
CHUNK = 4
MESH = pl.DeviceIdType.MESH
F32 = jnp.float32
BF16 = jnp.bfloat16


def mm(a, b):
    return jnp.dot(a, b, preferred_element_type=F32)


def mm_nt(a, b):
    return lax.dot_general(a, b, (((1,), (1,)), ((), ())), preferred_element_type=F32)


def mm_tn(a, b):
    return lax.dot_general(a, b, (((0,), (0,)), ((), ())), preferred_element_type=F32)


def kernel(
    tiles,
    dep_h, cnt_h, w_in_h, b_in_h, w_out_h, state_h, cot_h, local_h, remote_h,
    blocks_h, choice_h, din_h, db_h, dout_h,
    w_in, b_in, w_out, state, cot, local, remote, gy, result, patch,
    sendbox, fetched, outbox, returned, acc, racc, ysp, csp,
    gsum, dbsum, gout, gin, red, gall, dbin, xin, din, db, dout,
    ask_out, ask_in, spec_v, choice_v,
    dep, cnt, ask_s, spec_s, spot_s, prev_s,
    in_sem, chunk_sem, out_sem, end_sem, small_sem,
    ask_send, ask_recv, fet_send, fet_recv, ret_send, ret_recv,
    rs_send, rs_recv, db_send, db_recv, ag_send, ag_recv, x_send, x_recv,
):
    nblocks, width, feat = state.shape
    entries = remote.shape[0]
    nchunks = nblocks // CHUNK
    me = lax.axis_index("lon")
    group = min(GROUP, tiles)
    groups = tiles // group
    part = gout.shape[1]

    def peer_at(offset):
        return lax.rem(me + offset + tiles, tiles)

    loads = [
        pltpu.make_async_copy(src, dst, in_sem.at[n])
        for n, (src, dst) in enumerate([
            (dep_h, dep), (cnt_h, cnt), (state_h, state), (w_in_h, w_in), (b_in_h, b_in),
            (w_out_h, w_out), (remote_h, remote)])
    ]
    for copy in loads[:6]:
        copy.start()

    barrier = pltpu.get_barrier_semaphore()

    @pl.loop(1, tiles)
    def _(i):
        pl.semaphore_signal(barrier, inc=1, device_id={"lon": peer_at(i)}, device_id_type=MESH)

    def load_chunk(c):
        at = pl.ds(c * CHUNK, CHUNK)
        return (
            pltpu.make_async_copy(local_h.at[at], local.at[at], chunk_sem.at[0, c]),
            pltpu.make_async_copy(cot_h.at[at], cot.at[at], chunk_sem.at[1, c]),
        )

    @pl.loop(0, nchunks)
    def _(c):
        for copy in load_chunk(c):
            copy.start()

    loads[6].start()
    acc[0] = jnp.zeros((width, feat), F32)
    gsum[...] = jnp.zeros_like(gsum)
    dbsum[...] = jnp.zeros_like(dbsum)
    loads[0].wait()
    loads[1].wait()

    count = cnt[0]
    dests, spots = [], []
    line = lax.broadcasted_iota(jnp.int32, (8, 128), 0)
    lane = lax.broadcasted_iota(jnp.int32, (8, 128), 1)
    tile = jnp.full((8, 128), -1, jnp.int32)
    place = jnp.where(lane < CAP, line * CAP + lane, -1)
    slot_entry = jnp.full((8, 128), entries, jnp.int32)
    special = jnp.zeros((8, 128), jnp.int32)
    keys = []
    for e in range(entries):
        ahead = dep[0, e] - me
        ahead = jnp.where(ahead < -REACH, ahead + tiles, ahead)
        ahead = jnp.where(ahead > REACH, ahead - tiles, ahead)
        alive = e < count
        keys.append(jnp.where(alive, jnp.where(ahead > 0, 2 * ahead, jnp.maximum(-2 * ahead - 1, 0)), -1))
        dests.append(jnp.where(alive, dep[2, e], -1))
        rank = jnp.int32(0)
        for q in range(e):
            rank = rank + jnp.where(keys[q] == keys[e], 1, 0)
        spots.append(jnp.where(alive, keys[e] * CAP + rank, SLOTS))
        tile = jnp.where(place == spots[e], dep[1, e], tile)
    ask_out[...] = tile
    ask_in[0] = tile

    pl.semaphore_wait(barrier, tiles - 1)

    def ask_copy(r):
        return pltpu.make_async_remote_copy(
            src_ref=ask_out, dst_ref=ask_in.at[r],
            send_sem=ask_send.at[r], recv_sem=ask_recv.at[r],
            device_id={"lon": peer_at(OFFSETS[r])}, device_id_type=MESH)

    def fetch_copy(r):
        at = pl.ds(r * CAP, CAP)
        return pltpu.make_async_remote_copy(
            src_ref=sendbox.at[at], dst_ref=fetched.at[at],
            send_sem=fet_send.at[r], recv_sem=fet_recv.at[r],
            device_id={"lon": peer_at(-OFFSETS[r])}, device_id_type=MESH)

    def return_copy(r):
        at = pl.ds(r * CAP, CAP)
        return pltpu.make_async_remote_copy(
            src_ref=outbox.at[at], dst_ref=returned.at[at],
            send_sem=ret_send.at[r], recv_sem=ret_recv.at[r],
            device_id={"lon": peer_at(OFFSETS[r])}, device_id_type=MESH)

    far_first = list(range(SPAN - 1, 0, -1))
    for r in far_first:
        ask_copy(r).start()

    for e in range(entries):
        prev = jnp.int32(0)
        last = dests[e]
        for q in range(entries):
            if q != e:
                same = dests[q] == dests[e]
                prev = jnp.maximum(prev, jnp.where(same & (spots[q] < spots[e]), spots[q] + 1, 0))
                last = jnp.where(same & (spots[q] > spots[e]), -1, last)
        spot_s[e] = spots[e]
        prev_s[e] = prev
        slot_entry = jnp.where(lane == spots[e], e, slot_entry)
        special = jnp.where(lane == last, e + 1, special)
    spec_v[0] = special
    spec_v[1] = slot_entry
    spec_copy = pltpu.make_async_copy(spec_v, spec_s, small_sem.at[0])
    spec_copy.start()

    def network(y32, ct, marks):
        n = len(marks)
        y_b = y32.astype(BF16)
        pre = mm(y_b, w_in[...]) + b_in[...]
        hidden = jnp.tanh(pre)
        h_b = hidden.astype(BF16)
        ghid = mm_nt(ct, w_out[...])
        gpre = ghid * (1.0 - hidden * hidden)
        gpre_b = gpre.astype(BF16)
        ct32 = ct.astype(F32)
        out = (ct32 + mm_nt(gpre_b, w_in[...])).astype(BF16)
        y_m, ct_m, total = [], [], None
        for i in range(n):
            at = slice(i * width, (i + 1) * width)
            y_m.append((y32[at] * marks[i]).astype(BF16))
            ct_m.append((ct32[at] * marks[i]).astype(BF16))
            here = jnp.sum(gpre[at].reshape(width // 8, 8, -1), axis=0) * marks[i]
            total = here if total is None else total + here
        gsum[:feat] += mm_tn(jnp.concatenate(y_m, axis=0), gpre_b)
        gsum[feat:] += mm_tn(jnp.concatenate(ct_m, axis=0), h_b)
        dbsum[...] += total
        return out.reshape(n, width, feat)

    def step(c, carry):
        for copy in load_chunk(c):
            copy.wait()
        y, marks = [], []
        for i in range(CHUNK):
            t = c * CHUNK + i
            y.append(mm(local[t], state[t]))
            marks.append(jnp.where(spec_s[0, 0, t] == 0, 1.0, 0.0).astype(F32))
        ct = cot[pl.ds(c * CHUNK, CHUNK)].reshape(CHUNK * width, feat)
        gy[pl.ds(c * CHUNK, CHUNK)] = network(jnp.concatenate(y, axis=0), ct, marks)
        return carry

    for copy in loads[2:6]:
        copy.wait()
    spec_copy.wait()
    first = min(1, nchunks)
    lax.fori_loop(0, first, step, 0)

    for r in far_first:
        ask_copy(r).wait_recv()
    asked_copy = pltpu.make_async_copy(ask_in, ask_s, small_sem.at[1])
    asked_copy.start()
    asked_copy.wait()

    asked = [ask_s[r, r, c] for r in range(SPAN) for c in range(CAP)]
    for r in far_first + [0]:
        for k in range(r * CAP, (r + 1) * CAP):
            block = state[jnp.clip(asked[k], 0, nblocks - 1)]
            if r == 0:
                fetched[k] = block
            else:
                sendbox[k] = block
        if r != 0:
            fetch_copy(r).start()

    lax.fori_loop(first, nchunks, step, 0)

    for e in range(entries):
        d = dep[2, e]
        ysp[e] = mm(local[d], state[d])
        csp[e] = cot[d]
    loads[6].wait()
    choice = lane
    lasts = []
    for k in range(SLOTS):
        last = jnp.int32(SLOTS + k)
        for q in range(k):
            last = jnp.where(asked[q] == asked[k], q, last)
        lasts.append(last)
        choice = jnp.where(lane == asked[k], nblocks + k, choice)
    choice_v[...] = choice
    choice_copy = pltpu.make_async_copy(choice_v, choice_h, small_sem.at[2])
    choice_copy.start()

    for r in range(SPAN):
        if r != 0:
            fetch_copy(r).wait_recv()
        for k in range(r * CAP, (r + 1) * CAP):
            found = spec_s[1, 0, k]
            e = jnp.minimum(found, entries - 1)
            weight = jnp.where(found < entries, 1.0, 0.0).astype(F32)
            acc[k + 1] = mm(remote[e], fetched[k]) * weight + acc[prev_s[e]]

    @pl.loop(0, entries // CHUNK)
    def _(c):
        marks, y = [], []
        for i in range(CHUNK):
            e = c * CHUNK + i
            marks.append(jnp.where(spec_s[0, 0, dep[2, e]] == e + 1, 1.0, 0.0).astype(F32))
            y.append(ysp[e] + acc[jnp.minimum(spot_s[e], SLOTS - 1) + 1])
        ct = csp[pl.ds(c * CHUNK, CHUNK)].reshape(CHUNK * width, feat)
        gy[pl.ds(nblocks + c * CHUNK, CHUNK)] = network(jnp.concatenate(y, axis=0), ct, marks)

    mine = lax.rem(me, group)
    base = me - mine
    gout[...] = gsum[...].astype(BF16).reshape(gout.shape)
    dbin[me] = jnp.sum(dbsum[...], axis=0, keepdims=True)

    def mate(i):
        return lax.rem(mine + i, group)

    def share_copy(i):
        return pltpu.make_async_remote_copy(
            src_ref=gout.at[mate(i)], dst_ref=gin.at[i],
            send_sem=rs_send.at[i], recv_sem=rs_recv.at[i],
            device_id={"lon": base + mate(i)}, device_id_type=MESH)

    def bias_copy(i):
        return pltpu.make_async_remote_copy(
            src_ref=dbin.at[me], dst_ref=dbin.at[me],
            send_sem=db_send.at[i], recv_sem=db_recv.at[i],
            device_id={"lon": peer_at(i)}, device_id_type=MESH)

    def gather_copy(i):
        return pltpu.make_async_remote_copy(
            src_ref=red, dst_ref=gall.at[mine],
            send_sem=ag_send.at[i], recv_sem=ag_recv.at[i],
            device_id={"lon": base + mate(i)}, device_id_type=MESH)

    def cross_copy(i):
        return pltpu.make_async_remote_copy(
            src_ref=xin.at[me // group], dst_ref=xin.at[me // group],
            send_sem=x_send.at[i], recv_sem=x_recv.at[i],
            device_id={"lon": peer_at(i * group)}, device_id_type=MESH)

    @pl.loop(1, group)
    def _(i):
        share_copy(i).start()

    for r in far_first + [0]:
        for k in range(r * CAP, (r + 1) * CAP):
            e = jnp.minimum(spec_s[1, 0, k], entries - 1)
            at = jnp.maximum(spec_s[0, 0, dep[2, e]] - 1, 0) + nblocks
            value = mm_tn(remote[e], gy[at]).astype(BF16)
            if r == 0:
                returned[k] = value
            else:
                outbox[k] = value
        if r != 0:
            return_copy(r).start()

    @pl.loop(1, tiles)
    def _(i):
        bias_copy(i).start()

    def adjoint(t):
        s = spec_s[0, 0, t]
        return mm_tn(local[t], gy[jnp.where(s == 0, t, nblocks + s - 1)])

    def store_chunk(c):
        at = pl.ds(c * CHUNK, CHUNK)
        return pltpu.make_async_copy(result.at[at], blocks_h.at[at], out_sem.at[c])

    @pl.loop(0, nchunks)
    def _(c):
        for i in range(CHUNK):
            t = c * CHUNK + i
            result[t] = adjoint(t).astype(BF16)
        store_chunk(c).start()

    @pl.loop(1, group)
    def _(i):
        share_copy(i).wait_recv()

    share = gsum[pl.ds(pl.multiple_of(mine * part, part), part)]
    share = lax.fori_loop(1, group, lambda i, s: s + gin[i].astype(F32), share)
    if groups > 1:
        xin[me // group] = share.astype(BF16)

        @pl.loop(1, groups)
        def _(i):
            cross_copy(i).start()

        @pl.loop(1, groups)
        def _(i):
            cross_copy(i).wait()

        share = lax.fori_loop(
            0, groups, lambda i, s: s + xin[i].astype(F32), jnp.zeros(share.shape, F32))
    red[...] = share.astype(BF16)
    gall[mine] = share.astype(BF16)

    @pl.loop(1, group)
    def _(i):
        gather_copy(i).start()

    for k in range(SLOTS):
        racc[SLOTS + k] = adjoint(jnp.clip(asked[k], 0, nblocks - 1))
    for r in range(SPAN):
        if r != 0:
            return_copy(r).wait_recv()
        for k in range(r * CAP, (r + 1) * CAP):
            total = returned[k].astype(F32) + racc[lasts[k]]
            racc[k] = total
            patch[k] = total.astype(BF16)
    ends = [pltpu.make_async_copy(patch, blocks_h.at[pl.ds(nblocks, SLOTS)], end_sem.at[0])]
    ends[0].start()

    @pl.loop(1, tiles)
    def _(i):
        bias_copy(i).wait()

    db[...] = lax.fori_loop(1, tiles, lambda i, s: s + dbin[i], dbin[0])

    @pl.loop(1, group)
    def _(i):
        gather_copy(i).wait_recv()

    whole = gall[...].astype(F32).reshape(2 * feat, -1)
    din[...] = whole[:feat]
    dout[...] = whole[feat:].T
    for n, (src, dst) in enumerate([(db, db_h), (din, din_h), (dout, dout_h)]):
        ends.append(pltpu.make_async_copy(src, dst, end_sem.at[n + 1]))
        ends[-1].start()

    @pl.loop(1, group)
    def _(i):
        share_copy(i).wait_send()
        gather_copy(i).wait_send()

    for r in far_first:
        ask_copy(r).wait_send()
        fetch_copy(r).wait_send()
        return_copy(r).wait_send()

    @pl.loop(0, nchunks)
    def _(c):
        store_chunk(c).wait()

    choice_copy.wait()
    for copy in ends:
        copy.wait()


def finish(choice_h, blocks_h, din_h, db_h, dout_h, grad_h, din_o, db_o, dout_o,
           choice, blocks, din, db, dout, load_sem, store_sem, block_sem):
    loads = [
        pltpu.make_async_copy(src, dst, load_sem.at[n])
        for n, (src, dst) in enumerate([
            (choice_h, choice), (blocks_h, blocks), (din_h, din), (db_h, db), (dout_h, dout)])
    ]
    stores = [
        pltpu.make_async_copy(src, dst, store_sem.at[n])
        for n, (src, dst) in enumerate([(din, din_o), (db, db_o), (dout, dout_o)])
    ]
    for copy in loads:
        copy.start()
    for load, store in zip(loads[2:], stores):
        load.wait()
        store.start()
    loads[0].wait()
    loads[1].wait()
    nblocks = grad_h.shape[0]

    def move(t):
        return pltpu.make_async_copy(blocks.at[choice[0, t]], grad_h.at[t], block_sem.at[t])

    @pl.loop(0, nblocks, unroll=4)
    def _(t):
        move(t).start()

    for copy in stores:
        copy.wait()

    @pl.loop(0, nblocks, unroll=4)
    def _(t):
        move(t).wait()


def body(tiles, state, cotangent, local_interp, remote_interp, departures, counts, w_in, b_in, w_out):
    nblocks, width, _ = local_interp.shape
    feat = state.shape[1]
    hid = w_in.shape[1]
    entries = remote_interp.shape[0]
    nchunks = nblocks // CHUNK
    group = min(GROUP, tiles)
    part = 2 * feat // group
    dma = pltpu.SemaphoreType.DMA
    hbm = pl.BlockSpec(memory_space=pl.ANY)
    blk = (width, feat)
    grads = (
        jax.ShapeDtypeStruct((feat, hid), F32),
        jax.ShapeDtypeStruct((1, hid), F32),
        jax.ShapeDtypeStruct((hid, feat), F32),
    )
    blocks, choice, d_in, d_b, d_out = pl.pallas_call(
        functools.partial(kernel, tiles),
        out_shape=(
            jax.ShapeDtypeStruct((nblocks + SLOTS,) + blk, BF16),
            jax.ShapeDtypeStruct((8, 128), jnp.int32),
        ) + grads,
        in_specs=[hbm] * 9,
        out_specs=(hbm,) * 5,
        scratch_shapes=[
            pltpu.VMEM((feat, hid), BF16),
            pltpu.VMEM((1, hid), F32),
            pltpu.VMEM((hid, feat), BF16),
            pltpu.VMEM((nblocks,) + blk, BF16),
            pltpu.VMEM((nblocks,) + blk, BF16),
            pltpu.VMEM((nblocks, width, width), BF16),
            pltpu.VMEM((entries, width, width), BF16),
            pltpu.VMEM((nblocks + entries,) + blk, BF16),
            pltpu.VMEM((nblocks,) + blk, BF16),
            pltpu.VMEM((SLOTS,) + blk, BF16),
            pltpu.VMEM((SLOTS,) + blk, BF16),
            pltpu.VMEM((SLOTS,) + blk, BF16),
            pltpu.VMEM((SLOTS,) + blk, BF16),
            pltpu.VMEM((SLOTS,) + blk, BF16),
            pltpu.VMEM((SLOTS + 1,) + blk, F32),
            pltpu.VMEM((2 * SLOTS,) + blk, F32),
            pltpu.VMEM((entries,) + blk, F32),
            pltpu.VMEM((entries,) + blk, BF16),
            pltpu.VMEM((2 * feat, hid), F32),
            pltpu.VMEM((8, hid), F32),
            pltpu.VMEM((group, part, hid), BF16),
            pltpu.VMEM((group, part, hid), BF16),
            pltpu.VMEM((part, hid), BF16),
            pltpu.VMEM((group, part, hid), BF16),
            pltpu.VMEM((tiles, 1, hid), F32),
            pltpu.VMEM((tiles // group, part, hid), BF16),
            pltpu.VMEM((feat, hid), F32),
            pltpu.VMEM((1, hid), F32),
            pltpu.VMEM((hid, feat), F32),
            pltpu.VMEM((8, 128), jnp.int32),
            pltpu.VMEM((SPAN, 8, 128), jnp.int32),
            pltpu.VMEM((2, 8, 128), jnp.int32),
            pltpu.VMEM((8, 128), jnp.int32),
            pltpu.SMEM(departures.shape, jnp.int32),
            pltpu.SMEM(counts.shape, jnp.int32),
            pltpu.SMEM((SPAN, 8, 128), jnp.int32),
            pltpu.SMEM((2, 8, 128), jnp.int32),
            pltpu.SMEM((entries,), jnp.int32),
            pltpu.SMEM((entries,), jnp.int32),
            dma((7,)), dma((2, nchunks)), dma((nchunks,)), dma((4,)), dma((3,)),
            dma((SPAN,)), dma((SPAN,)), dma((SPAN,)), dma((SPAN,)), dma((SPAN,)), dma((SPAN,)),
            dma((group,)), dma((group,)), dma((tiles,)), dma((tiles,)),
            dma((group,)), dma((group,)),
            dma((max(tiles // group, 2),)), dma((max(tiles // group, 2),)),
        ],
        compiler_params=pltpu.CompilerParams(
            collective_id=0, has_side_effects=True, vmem_limit_bytes=63 * 1024 * 1024
        ),
    )(
        departures, counts, w_in, b_in.reshape(1, hid), w_out,
        state.reshape(nblocks, width, feat), cotangent.reshape(nblocks, width, feat),
        local_interp, remote_interp,
    )
    grad, d_in, d_b, d_out = pl.pallas_call(
        finish,
        out_shape=(jax.ShapeDtypeStruct((nblocks,) + blk, BF16),) + grads,
        in_specs=[hbm] * 5,
        out_specs=(hbm,) * 4,
        scratch_shapes=[
            pltpu.SMEM((8, 128), jnp.int32),
            pltpu.VMEM((nblocks + SLOTS,) + blk, BF16),
            pltpu.VMEM((feat, hid), F32),
            pltpu.VMEM((1, hid), F32),
            pltpu.VMEM((hid, feat), F32),
            dma((5,)), dma((3,)), dma((nblocks,)),
        ],
        compiler_params=pltpu.CompilerParams(vmem_limit_bytes=63 * 1024 * 1024),
    )(choice, blocks, d_in, d_b, d_out)
    return grad.reshape(nblocks * width, feat), d_in, d_b.reshape(hid), d_out


def solution(mesh):
    return jax.shard_map(
        functools.partial(body, mesh.shape["lon"]),
        mesh=mesh,
        in_specs=(
            P(("members", "lon"), None),
            P(("members", "lon"), None),
            P(("members", "lon"), None, None),
            P(("members", "lon"), None, None),
            P(None, ("members", "lon")),
            P(("members", "lon")),
            P(),
            P(),
            P(),
        ),
        out_specs=(
            P(("members", "lon"), None),
            P("members", None),
            P("members"),
            P("members", None),
        ),
        check_vma=False,
    )
```

```python
import functools

import jax
import jax.numpy as jnp
from jax import lax
from jax.experimental import pallas as pl
from jax.experimental.pallas import tpu as pltpu
from jax.sharding import PartitionSpec as P

CAP = 2
REACH = 3
SPAN = 2 * REACH + 1
OFFSETS = [0] + [sign * d for d in range(1, REACH + 1) for sign in (-1, 1)]
SLOTS = SPAN * CAP
GROUP = 16
CHUNK = 8
LIST_STEPS = 1
MARKS = (0, 2, 2, 6)
PIECES = 4
MESH = pl.DeviceIdType.MESH
F32 = jnp.float32
BF16 = jnp.bfloat16


def mm(a, b):
    return jnp.dot(a, b, preferred_element_type=F32)


def mm_nt(a, b):
    return lax.dot_general(a, b, (((1,), (1,)), ((), ())), preferred_element_type=F32)


def mm_tn(a, b):
    return lax.dot_general(a, b, (((0,), (0,)), ((), ())), preferred_element_type=F32)


def kernel(
    tiles,
    dep_h, cnt_h, w_in_h, b_in_h, w_out_h, state_h, cot_h, local_h, remote_h,
    blocks_h, choice_h, din_h, db_h, dout_h,
    w_in, b_in, w_out, state, cot, local, remote, gy, result, patch,
    sendbox, fetched, outbox, returned, acc, racc, ysp, csp,
    gsum, dbsum, gout, gin, red, gall, dbin, xin, din, db, dout,
    ask_out, ask_in, spec_v, choice_v,
    dep, cnt, ask_s, spec_s, spot_s, prev_s,
    in_sem, chunk_sem, out_sem, end_sem, small_sem,
    ask_send, ask_recv, fet_send, fet_recv, ret_send, ret_recv,
    rs_send, rs_recv, db_send, db_recv, ag_send, ag_recv, x_send, x_recv,
):
    nblocks, width, feat = state.shape
    entries = remote.shape[0]
    nchunks = nblocks // CHUNK
    me = lax.axis_index("lon")
    group = min(GROUP, tiles)
    groups = tiles // group
    part = gout.shape[1]

    def peer_at(offset):
        return lax.rem(me + offset + tiles, tiles)

    loads = [
        pltpu.make_async_copy(src, dst, in_sem.at[n])
        for n, (src, dst) in enumerate([
            (dep_h, dep), (cnt_h, cnt), (state_h, state), (w_in_h, w_in), (b_in_h, b_in),
            (w_out_h, w_out), (remote_h, remote)])
    ]
    for copy in loads[:6]:
        copy.start()

    barrier = pltpu.get_barrier_semaphore()

    @pl.loop(1, tiles)
    def _(i):
        pl.semaphore_signal(barrier, inc=1, device_id={"lon": peer_at(i)}, device_id_type=MESH)

    def load_chunk(c):
        at = pl.ds(c * CHUNK, CHUNK)
        return (
            pltpu.make_async_copy(local_h.at[at], local.at[at], chunk_sem.at[0, c]),
            pltpu.make_async_copy(cot_h.at[at], cot.at[at], chunk_sem.at[1, c]),
        )

    @pl.loop(0, nchunks)
    def _(c):
        for copy in load_chunk(c):
            copy.start()

    loads[6].start()
    acc[0] = jnp.zeros((width, feat), F32)
    gsum[...] = jnp.zeros_like(gsum)
    dbsum[...] = jnp.zeros_like(dbsum)
    loads[0].wait()
    loads[1].wait()

    count = cnt[0]
    dests, spots = [], []
    line = lax.broadcasted_iota(jnp.int32, (8, 128), 0)
    lane = lax.broadcasted_iota(jnp.int32, (8, 128), 1)
    tile = jnp.full((8, 128), -1, jnp.int32)
    place = jnp.where(lane < CAP, line * CAP + lane, -1)
    slot_entry = jnp.full((8, 128), entries, jnp.int32)
    special = jnp.zeros((8, 128), jnp.int32)
    keys = []
    for e in range(entries):
        ahead = dep[0, e] - me
        ahead = jnp.where(ahead < -REACH, ahead + tiles, ahead)
        ahead = jnp.where(ahead > REACH, ahead - tiles, ahead)
        alive = e < count
        keys.append(jnp.where(alive, jnp.where(ahead > 0, 2 * ahead, jnp.maximum(-2 * ahead - 1, 0)), -1))
        dests.append(jnp.where(alive, dep[2, e], -1))
        rank = jnp.int32(0)
        for q in range(e):
            rank = rank + jnp.where(keys[q] == keys[e], 1, 0)
        spots.append(jnp.where(alive, keys[e] * CAP + rank, SLOTS))
        tile = jnp.where(place == spots[e], dep[1, e], tile)
    ask_out[...] = tile
    ask_in[0] = tile

    for e in range(entries):
        prev = jnp.int32(0)
        last = dests[e]
        for q in range(entries):
            if q != e:
                same = dests[q] == dests[e]
                prev = jnp.maximum(prev, jnp.where(same & (spots[q] < spots[e]), spots[q] + 1, 0))
                last = jnp.where(same & (spots[q] > spots[e]), -1, last)
        spot_s[e] = spots[e]
        prev_s[e] = prev
        slot_entry = jnp.where(lane == spots[e], e, slot_entry)
        special = jnp.where(lane == last, e + 1, special)
    spec_v[0] = special
    spec_v[1] = slot_entry
    spec_copy = pltpu.make_async_copy(spec_v, spec_s, small_sem.at[0])
    spec_copy.start()

    def network(y32, ct, marks):
        n = len(marks)
        y_b = y32.astype(BF16)
        pre = mm(y_b, w_in[...]) + b_in[...]
        hidden = jnp.tanh(pre)
        h_b = hidden.astype(BF16)
        ghid = mm_nt(ct, w_out[...])
        gpre = ghid * (1.0 - hidden * hidden)
        gpre_b = gpre.astype(BF16)
        ct32 = ct.astype(F32)
        out = (ct32 + mm_nt(gpre_b, w_in[...])).astype(BF16)
        y_m, ct_m, total = [], [], None
        for i in range(n):
            at = slice(i * width, (i + 1) * width)
            y_m.append((y32[at] * marks[i]).astype(BF16))
            ct_m.append((ct32[at] * marks[i]).astype(BF16))
            here = jnp.sum(gpre[at].reshape(width // 8, 8, -1), axis=0) * marks[i]
            total = here if total is None else total + here
        gsum[:feat] += mm_tn(jnp.concatenate(y_m, axis=0), gpre_b)
        gsum[feat:] += mm_tn(jnp.concatenate(ct_m, axis=0), h_b)
        dbsum[...] += total
        return out.reshape(n, width, feat)

    def arrive(c):
        for copy in load_chunk(c):
            copy.wait()

    def step(c, carry, wait=True):
        if wait:
            arrive(c)
        y, marks = [], []
        for i in range(CHUNK):
            t = c * CHUNK + i
            y.append(mm(local[t], state[t]))
            marks.append(jnp.where(spec_s[0, 0, t] == 0, 1.0, 0.0).astype(F32))
        ct = cot[pl.ds(c * CHUNK, CHUNK)].reshape(CHUNK * width, feat)
        gy[pl.ds(c * CHUNK, CHUNK)] = network(jnp.concatenate(y, axis=0), ct, marks)
        return carry

    reach = [min(n, nchunks) for n in MARKS]
    for copy in loads[2:6]:
        copy.wait()
    spec_copy.wait()
    lax.fori_loop(0, reach[0], step, 0)

    pl.semaphore_wait(barrier, tiles - 1)

    def ask_copy(r):
        return pltpu.make_async_remote_copy(
            src_ref=ask_out, dst_ref=ask_in.at[r],
            send_sem=ask_send.at[r], recv_sem=ask_recv.at[r],
            device_id={"lon": peer_at(OFFSETS[r])}, device_id_type=MESH)

    def fetch_copy(r):
        at = pl.ds(r * CAP, CAP)
        return pltpu.make_async_remote_copy(
            src_ref=sendbox.at[at], dst_ref=fetched.at[at],
            send_sem=fet_send.at[r], recv_sem=fet_recv.at[r],
            device_id={"lon": peer_at(-OFFSETS[r])}, device_id_type=MESH)

    def return_copy(r):
        at = pl.ds(r * CAP, CAP)
        return pltpu.make_async_remote_copy(
            src_ref=outbox.at[at], dst_ref=returned.at[at],
            send_sem=ret_send.at[r], recv_sem=ret_recv.at[r],
            device_id={"lon": peer_at(OFFSETS[r])}, device_id_type=MESH)

    far_first = list(range(SPAN - 1, 0, -1))
    for r in far_first:
        ask_copy(r).start()

    lax.fori_loop(reach[0], reach[1], step, 0)
    for r in far_first:
        ask_copy(r).wait_recv()
    asked_copy = pltpu.make_async_copy(ask_in, ask_s, small_sem.at[1])
    asked_copy.start()
    lax.fori_loop(reach[1], reach[2], step, 0)
    asked_copy.wait()

    asked = [ask_s[r, r, c] for r in range(SPAN) for c in range(CAP)]
    for r in far_first + [0]:
        for k in range(r * CAP, (r + 1) * CAP):
            block = state[jnp.clip(asked[k], 0, nblocks - 1)]
            if r == 0:
                fetched[k] = block
            else:
                sendbox[k] = block
        if r != 0:
            fetch_copy(r).start()

    early = reach[3]
    lax.fori_loop(reach[2], early, step, 0)

    @pl.loop(early, nchunks)
    def _(c):
        arrive(c)

    for e in range(entries):
        d = dep[2, e]
        ysp[e] = mm(local[d], state[d])
        csp[e] = cot[d]
    loads[6].wait()
    choice = lane
    lasts = []
    for k in range(SLOTS):
        last = jnp.int32(SLOTS + k)
        for q in range(k):
            last = jnp.where(asked[q] == asked[k], q, last)
        lasts.append(last)
        choice = jnp.where(lane == asked[k], nblocks + k, choice)
    choice_v[...] = choice
    choice_copy = pltpu.make_async_copy(choice_v, choice_h, small_sem.at[2])
    choice_copy.start()

    for r in range(SPAN):
        if r != 0:
            fetch_copy(r).wait_recv()
        for k in range(r * CAP, (r + 1) * CAP):
            found = spec_s[1, 0, k]
            e = jnp.minimum(found, entries - 1)
            weight = jnp.where(found < entries, 1.0, 0.0).astype(F32)
            acc[k + 1] = mm(remote[e], fetched[k]) * weight + acc[prev_s[e]]

    few = entries // LIST_STEPS

    @pl.loop(0, LIST_STEPS)
    def _(c):
        marks, y = [], []
        for i in range(few):
            e = c * few + i
            marks.append(jnp.where(spec_s[0, 0, dep[2, e]] == e + 1, 1.0, 0.0).astype(F32))
            y.append(ysp[e] + acc[jnp.minimum(spot_s[e], SLOTS - 1) + 1])
        ct = csp[pl.ds(c * few, few)].reshape(few * width, feat)
        gy[pl.ds(nblocks + c * few, few)] = network(jnp.concatenate(y, axis=0), ct, marks)

    for r in far_first + [0]:
        for k in range(r * CAP, (r + 1) * CAP):
            e = jnp.minimum(spec_s[1, 0, k], entries - 1)
            at = jnp.maximum(spec_s[0, 0, dep[2, e]] - 1, 0) + nblocks
            value = mm_tn(remote[e], gy[at]).astype(BF16)
            if r == 0:
                returned[k] = value
            else:
                outbox[k] = value
        if r != 0:
            return_copy(r).start()

    lax.fori_loop(early, nchunks, functools.partial(step, wait=False), 0)

    mine = lax.rem(me, group)
    base = me - mine
    gout[...] = gsum[...].astype(BF16).reshape(gout.shape)
    dbin[me] = jnp.sum(dbsum[...], axis=0, keepdims=True)

    def mate(i):
        return lax.rem(mine + i, group)

    def share_copy(i):
        return pltpu.make_async_remote_copy(
            src_ref=gout.at[mate(i)], dst_ref=gin.at[i],
            send_sem=rs_send.at[i], recv_sem=rs_recv.at[i],
            device_id={"lon": base + mate(i)}, device_id_type=MESH)

    def bias_copy(i):
        return pltpu.make_async_remote_copy(
            src_ref=dbin.at[me], dst_ref=dbin.at[me],
            send_sem=db_send.at[i], recv_sem=db_recv.at[i],
            device_id={"lon": peer_at(i)}, device_id_type=MESH)

    def gather_copy(i):
        return pltpu.make_async_remote_copy(
            src_ref=red, dst_ref=gall.at[mine],
            send_sem=ag_send.at[i], recv_sem=ag_recv.at[i],
            device_id={"lon": base + mate(i)}, device_id_type=MESH)

    def cross_copy(i):
        return pltpu.make_async_remote_copy(
            src_ref=xin.at[me // group], dst_ref=xin.at[me // group],
            send_sem=x_send.at[i], recv_sem=x_recv.at[i],
            device_id={"lon": peer_at(i * group)}, device_id_type=MESH)

    @pl.loop(1, group)
    def _(i):
        share_copy(i).start()

    @pl.loop(1, tiles)
    def _(i):
        bias_copy(i).start()

    def adjoint(t):
        s = spec_s[0, 0, t]
        return mm_tn(local[t], gy[jnp.where(s == 0, t, nblocks + s - 1)])

    def store_chunk(c):
        at = pl.ds(c * CHUNK, CHUNK)
        return pltpu.make_async_copy(result.at[at], blocks_h.at[at], out_sem.at[c])

    @pl.loop(0, nchunks)
    def _(c):
        for i in range(CHUNK):
            t = c * CHUNK + i
            result[t] = adjoint(t).astype(BF16)
        store_chunk(c).start()

    @pl.loop(1, group)
    def _(i):
        share_copy(i).wait_recv()

    share = gsum[pl.ds(pl.multiple_of(mine * part, part), part)]
    share = lax.fori_loop(1, group, lambda i, s: s + gin[i].astype(F32), share)
    if groups > 1:
        xin[me // group] = share.astype(BF16)

        @pl.loop(1, groups)
        def _(i):
            cross_copy(i).start()

        @pl.loop(1, groups)
        def _(i):
            cross_copy(i).wait()

        share = lax.fori_loop(
            0, groups, lambda i, s: s + xin[i].astype(F32), jnp.zeros(share.shape, F32))
    red[...] = share.astype(BF16)
    gall[mine] = share.astype(BF16)

    @pl.loop(1, group)
    def _(i):
        gather_copy(i).start()

    for k in range(SLOTS):
        racc[SLOTS + k] = adjoint(jnp.clip(asked[k], 0, nblocks - 1))
    for r in range(SPAN):
        if r != 0:
            return_copy(r).wait_recv()
        for k in range(r * CAP, (r + 1) * CAP):
            total = returned[k].astype(F32) + racc[lasts[k]]
            racc[k] = total
            patch[k] = total.astype(BF16)
    ends = [pltpu.make_async_copy(patch, blocks_h.at[pl.ds(nblocks, SLOTS)], end_sem.at[0])]
    ends[0].start()

    @pl.loop(1, tiles)
    def _(i):
        bias_copy(i).wait()

    db[...] = lax.fori_loop(1, tiles, lambda i, s: s + dbin[i], dbin[0])

    @pl.loop(1, group)
    def _(i):
        gather_copy(i).wait_recv()

    whole = gall[...].astype(F32).reshape(2 * feat, -1)
    din[...] = whole[:feat]
    dout[...] = whole[feat:].T
    for n, (src, dst) in enumerate([(db, db_h), (din, din_h), (dout, dout_h)]):
        ends.append(pltpu.make_async_copy(src, dst, end_sem.at[n + 1]))
        ends[-1].start()

    @pl.loop(1, group)
    def _(i):
        share_copy(i).wait_send()
        gather_copy(i).wait_send()

    for r in far_first:
        ask_copy(r).wait_send()
        fetch_copy(r).wait_send()
        return_copy(r).wait_send()

    @pl.loop(0, nchunks)
    def _(c):
        store_chunk(c).wait()

    choice_copy.wait()
    for copy in ends:
        copy.wait()


def finish(choice_h, blocks_h, din_h, db_h, dout_h, grad_h, din_o, db_o, dout_o,
           choice, blocks, din, db, dout, load_sem, store_sem, part_sem, block_sem):
    nblocks = grad_h.shape[0]
    patches = pl.ds(nblocks, SLOTS)
    loads = [
        pltpu.make_async_copy(src, dst, load_sem.at[n])
        for n, (src, dst) in enumerate([
            (choice_h, choice), (blocks_h.at[patches], blocks.at[patches]),
            (din_h, din), (db_h, db), (dout_h, dout)])
    ]
    stores = [
        pltpu.make_async_copy(src, dst, store_sem.at[n])
        for n, (src, dst) in enumerate([(din, din_o), (db, db_o), (dout, dout_o)])
    ]
    piece = nblocks // PIECES

    def load_piece(p):
        at = pl.ds(p * piece, piece)
        return pltpu.make_async_copy(blocks_h.at[at], blocks.at[at], part_sem.at[p])

    def move(t):
        return pltpu.make_async_copy(blocks.at[choice[0, t]], grad_h.at[t], block_sem.at[t])

    for copy in loads[:2]:
        copy.start()
    for p in range(PIECES):
        load_piece(p).start()
    for copy in loads[2:]:
        copy.start()
    for copy in loads[:2]:
        copy.wait()
    for p in range(PIECES):
        load_piece(p).wait()

        @pl.loop(p * piece, (p + 1) * piece, unroll=4)
        def _(t):
            move(t).start()

    for load, store in zip(loads[2:], stores):
        load.wait()
        store.start()
    for copy in stores:
        copy.wait()

    @pl.loop(0, nblocks, unroll=4)
    def _(t):
        move(t).wait()


def body(tiles, state, cotangent, local_interp, remote_interp, departures, counts, w_in, b_in, w_out):
    nblocks, width, _ = local_interp.shape
    feat = state.shape[1]
    hid = w_in.shape[1]
    entries = remote_interp.shape[0]
    nchunks = nblocks // CHUNK
    group = min(GROUP, tiles)
    part = 2 * feat // group
    dma = pltpu.SemaphoreType.DMA
    hbm = pl.BlockSpec(memory_space=pl.ANY)
    blk = (width, feat)
    grads = (
        jax.ShapeDtypeStruct((feat, hid), F32),
        jax.ShapeDtypeStruct((1, hid), F32),
        jax.ShapeDtypeStruct((hid, feat), F32),
    )
    blocks, choice, d_in, d_b, d_out = pl.pallas_call(
        functools.partial(kernel, tiles),
        out_shape=(
            jax.ShapeDtypeStruct((nblocks + SLOTS,) + blk, BF16),
            jax.ShapeDtypeStruct((8, 128), jnp.int32),
        ) + grads,
        in_specs=[hbm] * 9,
        out_specs=(hbm,) * 5,
        scratch_shapes=[
            pltpu.VMEM((feat, hid), BF16),
            pltpu.VMEM((1, hid), F32),
            pltpu.VMEM((hid, feat), BF16),
            pltpu.VMEM((nblocks,) + blk, BF16),
            pltpu.VMEM((nblocks,) + blk, BF16),
            pltpu.VMEM((nblocks, width, width), BF16),
            pltpu.VMEM((entries, width, width), BF16),
            pltpu.VMEM((nblocks + entries,) + blk, BF16),
            pltpu.VMEM((nblocks,) + blk, BF16),
            pltpu.VMEM((SLOTS,) + blk, BF16),
            pltpu.VMEM((SLOTS,) + blk, BF16),
            pltpu.VMEM((SLOTS,) + blk, BF16),
            pltpu.VMEM((SLOTS,) + blk, BF16),
            pltpu.VMEM((SLOTS,) + blk, BF16),
            pltpu.VMEM((SLOTS + 1,) + blk, F32),
            pltpu.VMEM((2 * SLOTS,) + blk, F32),
            pltpu.VMEM((entries,) + blk, F32),
            pltpu.VMEM((entries,) + blk, BF16),
            pltpu.VMEM((2 * feat, hid), F32),
            pltpu.VMEM((8, hid), F32),
            pltpu.VMEM((group, part, hid), BF16),
            pltpu.VMEM((group, part, hid), BF16),
            pltpu.VMEM((part, hid), BF16),
            pltpu.VMEM((group, part, hid), BF16),
            pltpu.VMEM((tiles, 1, hid), F32),
            pltpu.VMEM((tiles // group, part, hid), BF16),
            pltpu.VMEM((feat, hid), F32),
            pltpu.VMEM((1, hid), F32),
            pltpu.VMEM((hid, feat), F32),
            pltpu.VMEM((8, 128), jnp.int32),
            pltpu.VMEM((SPAN, 8, 128), jnp.int32),
            pltpu.VMEM((2, 8, 128), jnp.int32),
            pltpu.VMEM((8, 128), jnp.int32),
            pltpu.SMEM(departures.shape, jnp.int32),
            pltpu.SMEM(counts.shape, jnp.int32),
            pltpu.SMEM((SPAN, 8, 128), jnp.int32),
            pltpu.SMEM((2, 8, 128), jnp.int32),
            pltpu.SMEM((entries,), jnp.int32),
            pltpu.SMEM((entries,), jnp.int32),
            dma((7,)), dma((2, nchunks)), dma((nchunks,)), dma((4,)), dma((3,)),
            dma((SPAN,)), dma((SPAN,)), dma((SPAN,)), dma((SPAN,)), dma((SPAN,)), dma((SPAN,)),
            dma((group,)), dma((group,)), dma((tiles,)), dma((tiles,)),
            dma((group,)), dma((group,)),
            dma((max(tiles // group, 2),)), dma((max(tiles // group, 2),)),
        ],
        compiler_params=pltpu.CompilerParams(
            collective_id=0, has_side_effects=True, vmem_limit_bytes=63 * 1024 * 1024
        ),
    )(
        departures, counts, w_in, b_in.reshape(1, hid), w_out,
        state.reshape(nblocks, width, feat), cotangent.reshape(nblocks, width, feat),
        local_interp, remote_interp,
    )
    grad, d_in, d_b, d_out = pl.pallas_call(
        finish,
        out_shape=(jax.ShapeDtypeStruct((nblocks,) + blk, BF16),) + grads,
        in_specs=[hbm] * 5,
        out_specs=(hbm,) * 4,
        scratch_shapes=[
            pltpu.SMEM((8, 128), jnp.int32),
            pltpu.VMEM((nblocks + SLOTS,) + blk, BF16),
            pltpu.VMEM((feat, hid), F32),
            pltpu.VMEM((1, hid), F32),
            pltpu.VMEM((hid, feat), F32),
            dma((5,)), dma((3,)), dma((PIECES,)), dma((nblocks,)),
        ],
        compiler_params=pltpu.CompilerParams(vmem_limit_bytes=63 * 1024 * 1024),
    )(choice, blocks, d_in, d_b, d_out)
    return grad.reshape(nblocks * width, feat), d_in, d_b.reshape(hid), d_out


def solution(mesh):
    return jax.shard_map(
        functools.partial(body, mesh.shape["lon"]),
        mesh=mesh,
        in_specs=(
            P(("members", "lon"), None),
            P(("members", "lon"), None),
            P(("members", "lon"), None, None),
            P(("members", "lon"), None, None),
            P(None, ("members", "lon")),
            P(("members", "lon")),
            P(),
            P(),
            P(),
        ),
        out_specs=(
            P(("members", "lon"), None),
            P("members", None),
            P("members"),
            P("members", None),
        ),
        check_vma=False,
    )
```

```python
import functools

import jax
import jax.numpy as jnp
from jax import lax
from jax.experimental import pallas as pl
from jax.experimental.pallas import tpu as pltpu
from jax.sharding import PartitionSpec as P

CAP = 2
REACH = 3
SPAN = 2 * REACH + 1
OFFSETS = [0] + [sign * d for d in range(1, REACH + 1) for sign in (-1, 1)]
SLOTS = SPAN * CAP
GROUP = 16
CHUNK = 8
LIST_STEPS = 1
MARKS = (0, 2, 2, 7)
PIECES = 4
MESH = pl.DeviceIdType.MESH
F32 = jnp.float32
BF16 = jnp.bfloat16


def mm(a, b):
    return jnp.dot(a, b, preferred_element_type=F32)


def mm_nt(a, b):
    return lax.dot_general(a, b, (((1,), (1,)), ((), ())), preferred_element_type=F32)


def mm_tn(a, b):
    return lax.dot_general(a, b, (((0,), (0,)), ((), ())), preferred_element_type=F32)


def kernel(
    tiles,
    dep_h, cnt_h, w_in_h, b_in_h, w_out_h, state_h, cot_h, local_h, remote_h,
    blocks_h, choice_h, din_h, db_h, dout_h,
    w_in, b_in, w_out, state, cot, local, remote, gy, result, patch,
    sendbox, fetched, outbox, returned, acc, racc, ysp, csp,
    gsum, dbsum, gout, gin, red, gall, dbin, xin, din, db, dout,
    ask_out, ask_in, spec_v, choice_v,
    dep, cnt, ask_s, spec_s, spot_s, prev_s,
    in_sem, chunk_sem, out_sem, end_sem, small_sem,
    ask_send, ask_recv, fet_send, fet_recv, ret_send, ret_recv,
    rs_send, rs_recv, db_send, db_recv, ag_send, ag_recv, x_send, x_recv,
):
    nblocks, width, feat = state.shape
    entries = remote.shape[0]
    nchunks = nblocks // CHUNK
    me = lax.axis_index("lon")
    group = min(GROUP, tiles)
    groups = tiles // group
    part = gout.shape[1]

    def peer_at(offset):
        return lax.rem(me + offset + tiles, tiles)

    loads = [
        pltpu.make_async_copy(src, dst, in_sem.at[n])
        for n, (src, dst) in enumerate([
            (dep_h, dep), (cnt_h, cnt), (state_h, state), (w_in_h, w_in), (b_in_h, b_in),
            (w_out_h, w_out), (remote_h, remote)])
    ]
    for copy in loads[:6]:
        copy.start()

    barrier = pltpu.get_barrier_semaphore()

    @pl.loop(1, tiles)
    def _(i):
        pl.semaphore_signal(barrier, inc=1, device_id={"lon": peer_at(i)}, device_id_type=MESH)

    def load_chunk(c):
        at = pl.ds(c * CHUNK, CHUNK)
        return (
            pltpu.make_async_copy(local_h.at[at], local.at[at], chunk_sem.at[0, c]),
            pltpu.make_async_copy(cot_h.at[at], cot.at[at], chunk_sem.at[1, c]),
        )

    @pl.loop(0, nchunks)
    def _(c):
        for copy in load_chunk(c):
            copy.start()

    loads[6].start()
    acc[0] = jnp.zeros((width, feat), F32)
    gsum[...] = jnp.zeros_like(gsum)
    dbsum[...] = jnp.zeros_like(dbsum)
    loads[0].wait()
    loads[1].wait()

    count = cnt[0]
    dests, spots = [], []
    line = lax.broadcasted_iota(jnp.int32, (8, 128), 0)
    lane = lax.broadcasted_iota(jnp.int32, (8, 128), 1)
    tile = jnp.full((8, 128), -1, jnp.int32)
    place = jnp.where(lane < CAP, line * CAP + lane, -1)
    slot_entry = jnp.full((8, 128), entries, jnp.int32)
    special = jnp.zeros((8, 128), jnp.int32)
    keys = []
    for e in range(entries):
        ahead = dep[0, e] - me
        ahead = jnp.where(ahead < -REACH, ahead + tiles, ahead)
        ahead = jnp.where(ahead > REACH, ahead - tiles, ahead)
        alive = e < count
        keys.append(jnp.where(alive, jnp.where(ahead > 0, 2 * ahead, jnp.maximum(-2 * ahead - 1, 0)), -1))
        dests.append(jnp.where(alive, dep[2, e], -1))
        rank = jnp.int32(0)
        for q in range(e):
            rank = rank + jnp.where(keys[q] == keys[e], 1, 0)
        spots.append(jnp.where(alive, keys[e] * CAP + rank, SLOTS))
        tile = jnp.where(place == spots[e], dep[1, e], tile)
    ask_out[...] = tile
    ask_in[0] = tile

    for e in range(entries):
        prev = jnp.int32(0)
        last = dests[e]
        for q in range(entries):
            if q != e:
                same = dests[q] == dests[e]
                prev = jnp.maximum(prev, jnp.where(same & (spots[q] < spots[e]), spots[q] + 1, 0))
                last = jnp.where(same & (spots[q] > spots[e]), -1, last)
        spot_s[e] = spots[e]
        prev_s[e] = prev
        slot_entry = jnp.where(lane == spots[e], e, slot_entry)
        special = jnp.where(lane == last, e + 1, special)
    spec_v[0] = special
    spec_v[1] = slot_entry
    spec_copy = pltpu.make_async_copy(spec_v, spec_s, small_sem.at[0])
    spec_copy.start()

    def network(y32, ct, marks):
        n = len(marks)
        y_b = y32.astype(BF16)
        pre = mm(y_b, w_in[...]) + b_in[...]
        hidden = jnp.tanh(pre)
        h_b = hidden.astype(BF16)
        ghid = mm_nt(ct, w_out[...])
        gpre = ghid * (1.0 - hidden * hidden)
        gpre_b = gpre.astype(BF16)
        ct32 = ct.astype(F32)
        out = (ct32 + mm_nt(gpre_b, w_in[...])).astype(BF16)
        y_m, ct_m, total = [], [], None
        for i in range(n):
            at = slice(i * width, (i + 1) * width)
            y_m.append((y32[at] * marks[i]).astype(BF16))
            ct_m.append((ct32[at] * marks[i]).astype(BF16))
            here = jnp.sum(gpre[at].reshape(width // 8, 8, -1), axis=0) * marks[i]
            total = here if total is None else total + here
        gsum[:feat] += mm_tn(jnp.concatenate(y_m, axis=0), gpre_b)
        gsum[feat:] += mm_tn(jnp.concatenate(ct_m, axis=0), h_b)
        dbsum[...] += total
        return out.reshape(n, width, feat)

    def arrive(c):
        for copy in load_chunk(c):
            copy.wait()

    def step(c, carry, wait=True):
        if wait:
            arrive(c)
        y, marks = [], []
        for i in range(CHUNK):
            t = c * CHUNK + i
            y.append(mm(local[t], state[t]))
            marks.append(jnp.where(spec_s[0, 0, t] == 0, 1.0, 0.0).astype(F32))
        ct = cot[pl.ds(c * CHUNK, CHUNK)].reshape(CHUNK * width, feat)
        gy[pl.ds(c * CHUNK, CHUNK)] = network(jnp.concatenate(y, axis=0), ct, marks)
        return carry

    reach = [min(n, nchunks) for n in MARKS]
    for copy in loads[2:6]:
        copy.wait()
    spec_copy.wait()
    lax.fori_loop(0, reach[0], step, 0)

    pl.semaphore_wait(barrier, tiles - 1)

    def ask_copy(r):
        return pltpu.make_async_remote_copy(
            src_ref=ask_out, dst_ref=ask_in.at[r],
            send_sem=ask_send.at[r], recv_sem=ask_recv.at[r],
            device_id={"lon": peer_at(OFFSETS[r])}, device_id_type=MESH)

    def fetch_copy(r):
        at = pl.ds(r * CAP, CAP)
        return pltpu.make_async_remote_copy(
            src_ref=sendbox.at[at], dst_ref=fetched.at[at],
            send_sem=fet_send.at[r], recv_sem=fet_recv.at[r],
            device_id={"lon": peer_at(-OFFSETS[r])}, device_id_type=MESH)

    def return_copy(r):
        at = pl.ds(r * CAP, CAP)
        return pltpu.make_async_remote_copy(
            src_ref=outbox.at[at], dst_ref=returned.at[at],
            send_sem=ret_send.at[r], recv_sem=ret_recv.at[r],
            device_id={"lon": peer_at(OFFSETS[r])}, device_id_type=MESH)

    far_first = list(range(SPAN - 1, 0, -1))
    for r in far_first:
        ask_copy(r).start()

    lax.fori_loop(reach[0], reach[1], step, 0)
    for r in far_first:
        ask_copy(r).wait_recv()
    asked_copy = pltpu.make_async_copy(ask_in, ask_s, small_sem.at[1])
    asked_copy.start()
    lax.fori_loop(reach[1], reach[2], step, 0)
    asked_copy.wait()

    asked = [ask_s[r, r, c] for r in range(SPAN) for c in range(CAP)]
    for r in far_first + [0]:
        for k in range(r * CAP, (r + 1) * CAP):
            block = state[jnp.clip(asked[k], 0, nblocks - 1)]
            if r == 0:
                fetched[k] = block
            else:
                sendbox[k] = block
        if r != 0:
            fetch_copy(r).start()

    early = reach[3]
    lax.fori_loop(reach[2], early, step, 0)

    @pl.loop(early, nchunks)
    def _(c):
        arrive(c)

    for e in range(entries):
        d = dep[2, e]
        ysp[e] = mm(local[d], state[d])
        csp[e] = cot[d]
    loads[6].wait()
    choice = lane
    lasts = []
    for k in range(SLOTS):
        last = jnp.int32(SLOTS + k)
        for q in range(k):
            last = jnp.where(asked[q] == asked[k], q, last)
        lasts.append(last)
        choice = jnp.where(lane == asked[k], nblocks + k, choice)
    choice_v[...] = choice
    choice_copy = pltpu.make_async_copy(choice_v, choice_h, small_sem.at[2])
    choice_copy.start()

    for r in range(SPAN):
        if r != 0:
            fetch_copy(r).wait_recv()
        for k in range(r * CAP, (r + 1) * CAP):
            found = spec_s[1, 0, k]
            e = jnp.minimum(found, entries - 1)
            weight = jnp.where(found < entries, 1.0, 0.0).astype(F32)
            acc[k + 1] = mm(remote[e], fetched[k]) * weight + acc[prev_s[e]]

    few = entries // LIST_STEPS

    @pl.loop(0, LIST_STEPS)
    def _(c):
        marks, y = [], []
        for i in range(few):
            e = c * few + i
            marks.append(jnp.where(spec_s[0, 0, dep[2, e]] == e + 1, 1.0, 0.0).astype(F32))
            y.append(ysp[e] + acc[jnp.minimum(spot_s[e], SLOTS - 1) + 1])
        ct = csp[pl.ds(c * few, few)].reshape(few * width, feat)
        gy[pl.ds(nblocks + c * few, few)] = network(jnp.concatenate(y, axis=0), ct, marks)

    lax.fori_loop(early, nchunks, functools.partial(step, wait=False), 0)

    mine = lax.rem(me, group)
    base = me - mine
    gout[...] = gsum[...].astype(BF16).reshape(gout.shape)
    dbin[me] = jnp.sum(dbsum[...], axis=0, keepdims=True)

    def mate(i):
        return lax.rem(mine + i, group)

    def share_copy(i):
        return pltpu.make_async_remote_copy(
            src_ref=gout.at[mate(i)], dst_ref=gin.at[i],
            send_sem=rs_send.at[i], recv_sem=rs_recv.at[i],
            device_id={"lon": base + mate(i)}, device_id_type=MESH)

    def bias_copy(i):
        return pltpu.make_async_remote_copy(
            src_ref=dbin.at[me], dst_ref=dbin.at[me],
            send_sem=db_send.at[i], recv_sem=db_recv.at[i],
            device_id={"lon": peer_at(i)}, device_id_type=MESH)

    def gather_copy(i):
        return pltpu.make_async_remote_copy(
            src_ref=red, dst_ref=gall.at[mine],
            send_sem=ag_send.at[i], recv_sem=ag_recv.at[i],
            device_id={"lon": base + mate(i)}, device_id_type=MESH)

    def cross_copy(i):
        return pltpu.make_async_remote_copy(
            src_ref=xin.at[me // group], dst_ref=xin.at[me // group],
            send_sem=x_send.at[i], recv_sem=x_recv.at[i],
            device_id={"lon": peer_at(i * group)}, device_id_type=MESH)

    @pl.loop(1, group)
    def _(i):
        share_copy(i).start()

    for r in far_first + [0]:
        for k in range(r * CAP, (r + 1) * CAP):
            e = jnp.minimum(spec_s[1, 0, k], entries - 1)
            at = jnp.maximum(spec_s[0, 0, dep[2, e]] - 1, 0) + nblocks
            value = mm_tn(remote[e], gy[at]).astype(BF16)
            if r == 0:
                returned[k] = value
            else:
                outbox[k] = value
        if r != 0:
            return_copy(r).start()

    @pl.loop(1, tiles)
    def _(i):
        bias_copy(i).start()

    def adjoint(t):
        s = spec_s[0, 0, t]
        return mm_tn(local[t], gy[jnp.where(s == 0, t, nblocks + s - 1)])

    def store_chunk(c):
        at = pl.ds(c * CHUNK, CHUNK)
        return pltpu.make_async_copy(result.at[at], blocks_h.at[at], out_sem.at[c])

    @pl.loop(0, nchunks)
    def _(c):
        for i in range(CHUNK):
            t = c * CHUNK + i
            result[t] = adjoint(t).astype(BF16)
        store_chunk(c).start()

    @pl.loop(1, group)
    def _(i):
        share_copy(i).wait_recv()

    share = gsum[pl.ds(pl.multiple_of(mine * part, part), part)]
    share = lax.fori_loop(1, group, lambda i, s: s + gin[i].astype(F32), share)
    if groups > 1:
        xin[me // group] = share.astype(BF16)

        @pl.loop(1, groups)
        def _(i):
            cross_copy(i).start()

        @pl.loop(1, groups)
        def _(i):
            cross_copy(i).wait()

        share = lax.fori_loop(
            0, groups, lambda i, s: s + xin[i].astype(F32), jnp.zeros(share.shape, F32))
    red[...] = share.astype(BF16)
    gall[mine] = share.astype(BF16)

    @pl.loop(1, group)
    def _(i):
        gather_copy(i).start()

    for k in range(SLOTS):
        racc[SLOTS + k] = adjoint(jnp.clip(asked[k], 0, nblocks - 1))
    for r in range(SPAN):
        if r != 0:
            return_copy(r).wait_recv()
        for k in range(r * CAP, (r + 1) * CAP):
            total = returned[k].astype(F32) + racc[lasts[k]]
            racc[k] = total
            patch[k] = total.astype(BF16)
    ends = [pltpu.make_async_copy(patch, blocks_h.at[pl.ds(nblocks, SLOTS)], end_sem.at[0])]
    ends[0].start()

    @pl.loop(1, tiles)
    def _(i):
        bias_copy(i).wait()

    db[...] = lax.fori_loop(1, tiles, lambda i, s: s + dbin[i], dbin[0])

    @pl.loop(1, group)
    def _(i):
        gather_copy(i).wait_recv()

    whole = gall[...].astype(F32).reshape(2 * feat, -1)
    din[...] = whole[:feat]
    dout[...] = whole[feat:].T
    for n, (src, dst) in enumerate([(db, db_h), (din, din_h), (dout, dout_h)]):
        ends.append(pltpu.make_async_copy(src, dst, end_sem.at[n + 1]))
        ends[-1].start()

    @pl.loop(1, group)
    def _(i):
        share_copy(i).wait_send()
        gather_copy(i).wait_send()

    for r in far_first:
        ask_copy(r).wait_send()
        fetch_copy(r).wait_send()
        return_copy(r).wait_send()

    @pl.loop(0, nchunks)
    def _(c):
        store_chunk(c).wait()

    choice_copy.wait()
    for copy in ends:
        copy.wait()


def finish(choice_h, blocks_h, din_h, db_h, dout_h, grad_h, din_o, db_o, dout_o,
           choice, blocks, din, db, dout, load_sem, store_sem, part_sem, block_sem):
    nblocks = grad_h.shape[0]
    patches = pl.ds(nblocks, SLOTS)
    loads = [
        pltpu.make_async_copy(src, dst, load_sem.at[n])
        for n, (src, dst) in enumerate([
            (choice_h, choice), (blocks_h.at[patches], blocks.at[patches]),
            (din_h, din), (db_h, db), (dout_h, dout)])
    ]
    stores = [
        pltpu.make_async_copy(src, dst, store_sem.at[n])
        for n, (src, dst) in enumerate([(din, din_o), (db, db_o), (dout, dout_o)])
    ]
    piece = nblocks // PIECES

    def load_piece(p):
        at = pl.ds(p * piece, piece)
        return pltpu.make_async_copy(blocks_h.at[at], blocks.at[at], part_sem.at[p])

    def move(t):
        return pltpu.make_async_copy(blocks.at[choice[0, t]], grad_h.at[t], block_sem.at[t])

    for copy in loads[:2]:
        copy.start()
    for p in range(PIECES):
        load_piece(p).start()
    for copy in loads[2:]:
        copy.start()
    for copy in loads[:2]:
        copy.wait()
    for p in range(PIECES):
        load_piece(p).wait()

        @pl.loop(p * piece, (p + 1) * piece, unroll=4)
        def _(t):
            move(t).start()

    for load, store in zip(loads[2:], stores):
        load.wait()
        store.start()
    for copy in stores:
        copy.wait()

    @pl.loop(0, nblocks, unroll=4)
    def _(t):
        move(t).wait()


def body(tiles, state, cotangent, local_interp, remote_interp, departures, counts, w_in, b_in, w_out):
    nblocks, width, _ = local_interp.shape
    feat = state.shape[1]
    hid = w_in.shape[1]
    entries = remote_interp.shape[0]
    nchunks = nblocks // CHUNK
    group = min(GROUP, tiles)
    part = 2 * feat // group
    dma = pltpu.SemaphoreType.DMA
    hbm = pl.BlockSpec(memory_space=pl.ANY)
    blk = (width, feat)
    grads = (
        jax.ShapeDtypeStruct((feat, hid), F32),
        jax.ShapeDtypeStruct((1, hid), F32),
        jax.ShapeDtypeStruct((hid, feat), F32),
    )
    blocks, choice, d_in, d_b, d_out = pl.pallas_call(
        functools.partial(kernel, tiles),
        out_shape=(
            jax.ShapeDtypeStruct((nblocks + SLOTS,) + blk, BF16),
            jax.ShapeDtypeStruct((8, 128), jnp.int32),
        ) + grads,
        in_specs=[hbm] * 9,
        out_specs=(hbm,) * 5,
        scratch_shapes=[
            pltpu.VMEM((feat, hid), BF16),
            pltpu.VMEM((1, hid), F32),
            pltpu.VMEM((hid, feat), BF16),
            pltpu.VMEM((nblocks,) + blk, BF16),
            pltpu.VMEM((nblocks,) + blk, BF16),
            pltpu.VMEM((nblocks, width, width), BF16),
            pltpu.VMEM((entries, width, width), BF16),
            pltpu.VMEM((nblocks + entries,) + blk, BF16),
            pltpu.VMEM((nblocks,) + blk, BF16),
            pltpu.VMEM((SLOTS,) + blk, BF16),
            pltpu.VMEM((SLOTS,) + blk, BF16),
            pltpu.VMEM((SLOTS,) + blk, BF16),
            pltpu.VMEM((SLOTS,) + blk, BF16),
            pltpu.VMEM((SLOTS,) + blk, BF16),
            pltpu.VMEM((SLOTS + 1,) + blk, F32),
            pltpu.VMEM((2 * SLOTS,) + blk, F32),
            pltpu.VMEM((entries,) + blk, F32),
            pltpu.VMEM((entries,) + blk, BF16),
            pltpu.VMEM((2 * feat, hid), F32),
            pltpu.VMEM((8, hid), F32),
            pltpu.VMEM((group, part, hid), BF16),
            pltpu.VMEM((group, part, hid), BF16),
            pltpu.VMEM((part, hid), BF16),
            pltpu.VMEM((group, part, hid), BF16),
            pltpu.VMEM((tiles, 1, hid), F32),
            pltpu.VMEM((tiles // group, part, hid), BF16),
            pltpu.VMEM((feat, hid), F32),
            pltpu.VMEM((1, hid), F32),
            pltpu.VMEM((hid, feat), F32),
            pltpu.VMEM((8, 128), jnp.int32),
            pltpu.VMEM((SPAN, 8, 128), jnp.int32),
            pltpu.VMEM((2, 8, 128), jnp.int32),
            pltpu.VMEM((8, 128), jnp.int32),
            pltpu.SMEM(departures.shape, jnp.int32),
            pltpu.SMEM(counts.shape, jnp.int32),
            pltpu.SMEM((SPAN, 8, 128), jnp.int32),
            pltpu.SMEM((2, 8, 128), jnp.int32),
            pltpu.SMEM((entries,), jnp.int32),
            pltpu.SMEM((entries,), jnp.int32),
            dma((7,)), dma((2, nchunks)), dma((nchunks,)), dma((4,)), dma((3,)),
            dma((SPAN,)), dma((SPAN,)), dma((SPAN,)), dma((SPAN,)), dma((SPAN,)), dma((SPAN,)),
            dma((group,)), dma((group,)), dma((tiles,)), dma((tiles,)),
            dma((group,)), dma((group,)),
            dma((max(tiles // group, 2),)), dma((max(tiles // group, 2),)),
        ],
        compiler_params=pltpu.CompilerParams(
            collective_id=0, has_side_effects=True, vmem_limit_bytes=63 * 1024 * 1024
        ),
    )(
        departures, counts, w_in, b_in.reshape(1, hid), w_out,
        state.reshape(nblocks, width, feat), cotangent.reshape(nblocks, width, feat),
        local_interp, remote_interp,
    )
    grad, d_in, d_b, d_out = pl.pallas_call(
        finish,
        out_shape=(jax.ShapeDtypeStruct((nblocks,) + blk, BF16),) + grads,
        in_specs=[hbm] * 5,
        out_specs=(hbm,) * 4,
        scratch_shapes=[
            pltpu.SMEM((8, 128), jnp.int32),
            pltpu.VMEM((nblocks + SLOTS,) + blk, BF16),
            pltpu.VMEM((feat, hid), F32),
            pltpu.VMEM((1, hid), F32),
            pltpu.VMEM((hid, feat), F32),
            dma((5,)), dma((3,)), dma((PIECES,)), dma((nblocks,)),
        ],
        compiler_params=pltpu.CompilerParams(vmem_limit_bytes=63 * 1024 * 1024),
    )(choice, blocks, d_in, d_b, d_out)
    return grad.reshape(nblocks * width, feat), d_in, d_b.reshape(hid), d_out


def solution(mesh):
    return jax.shard_map(
        functools.partial(body, mesh.shape["lon"]),
        mesh=mesh,
        in_specs=(
            P(("members", "lon"), None),
            P(("members", "lon"), None),
            P(("members", "lon"), None, None),
            P(("members", "lon"), None, None),
            P(None, ("members", "lon")),
            P(("members", "lon")),
            P(),
            P(),
            P(),
        ),
        out_specs=(
            P(("members", "lon"), None),
            P("members", None),
            P("members"),
            P("members", None),
        ),
        check_vma=False,
    )
```
